256 devices in a mesh: row: 32 (over y, x, core), col: 8 (over z).
Axes of the slice: x: 4, y: 4, z: 8, core: 2. Of those that a mesh axis runs over, the one named last changes fastest.
Arguments:
- features: bfloat16 [524288, 256], P(('row', 'col')), may hold values from -6 to 6
- w_self: bfloat16 [256, 256], replicated, may hold values from -0.375 to 0.375
- w_neigh: bfloat16 [256, 256], replicated, may hold values from -1.5 to 1.5
- bias: float32 [256], replicated, may hold values from -3 to 3
- hub_ids: int32 [6], replicated, may hold values from 0 to 31
- hub_adj: bfloat16 [256, 6, 2048, 256], P(('row', 'col')), may hold values from 0 to 2, as said below
- send_tile: int32 [256, 8, 2], P(('row', 'col')), may hold values from 0 to 15
- recv_count: int32 [256, 8], P(('row', 'col')), may hold values from 0 to 2, as said below
- recv_dst: int32 [256, 8, 2], P(('row', 'col')), may hold values from 0 to 15
- recv_adj: bfloat16 [256, 8, 2, 128, 128], P(('row', 'col')), may hold values from 0 to 2, as said below
- cotangent: bfloat16 [524288, 256], P(('row', 'col')), may hold values from -6 to 6
Outputs:
- output: bfloat16 [524288, 256], P(('row', 'col'))
- feature_grad: bfloat16 [524288, 256], P(('row', 'col'))
The draws below stay inside these ranges and needn't reach their ends.
Inputs may be any that keep to these rules, and one draw needn't show every extreme that they name: `recv_count`: every device uses all 2 slots from at least one device of its row group. `hub_adj`: nonnegative edge weights. `recv_adj`: nonnegative edge weights.
All inputs are finite; a program needn't handle non-finite values.
Results may differ from the reference program's by a relative error of at most 0.0055.
Values may be sent and summed in bfloat16 or wider, within the bound.
A program may use at most 64 MiB of HBM per device.

```python
import math
import jax
import jax.numpy as jnp
import numpy as np
from jax import lax

D = 256
OUT = 256
NODE_DEV = 2048
TILE = 128
HUB = 256
SECTIONS = 6
CAP = 2
NODES = 524288
BLOCKS = 256
N_ROW = 32
N_COL = 8


def draw_hub_adj(key, part):
    shape = (N_ROW * N_COL, SECTIONS, NODE_DEV, HUB)
    first, second = jax.random.split(jax.random.fold_in(key, 11))
    present = jax.random.uniform(first, shape) < 4.0 / HUB
    values = jnp.exp(jax.random.uniform(second, shape, minval=math.log(0.25), maxval=math.log(2.0)))
    return jnp.where(present, values, 0.0).astype(jnp.bfloat16)


def draw_recv_adj(key, part):
    shape = (N_ROW * N_COL, N_COL, CAP, TILE, TILE)
    first, second = jax.random.split(jax.random.fold_in(key, 23))
    present = jax.random.uniform(first, shape) < 4.0 / TILE
    values = jnp.exp(jax.random.uniform(second, shape, minval=math.log(0.25), maxval=math.log(2.0)))
    return jnp.where(present, values, 0.0).astype(jnp.bfloat16)


def draw_recv_count(key, part):
    first, second = jax.random.split(jax.random.fold_in(key, 37))
    base = jax.random.randint(first, (N_ROW * N_COL, N_COL), 0, CAP + 1)
    full_source = jax.random.randint(second, (N_ROW * N_COL, 1), 0, N_COL)
    positions = jnp.arange(N_COL, dtype=jnp.int32)[None, :]
    return jnp.where(positions == full_source, CAP, base).astype(jnp.int32)


def plant(result, key, smallest, high):
    longest = result.shape.index(max(result.shape))
    spots = []
    for shift in (0, 1):
        where = [jax.random.randint(jax.random.fold_in(key, axis), (), 0, length) for axis, length in enumerate(result.shape)]
        where[longest] = (where[longest] + shift) % result.shape[longest]
        spots.append(tuple(where))
    return result.at[spots[0]].set(smallest).at[spots[1]].set(high)


def level_of(own_key, extent, cuts, smallest, high):
    loudness, own = 1.0, jax.random.fold_in(own_key, 6)
    for position, blocks in cuts:
        steps = jnp.exp(jax.random.uniform(jax.random.fold_in(own, position), (blocks,), jnp.float32, smallest / len(cuts), high / len(cuts)))
        loudness = loudness * jnp.repeat(steps, extent[position] // blocks).reshape([-1 if axis == position else 1 for axis in range(len(extent))])
    return loudness


def rank_table(number_of, lean):
    loads = [(1 << 20) // math.isqrt(standing ** lean) + 1 for standing in range(1, number_of + 1)]
    spread = 1 + sum(loads) // (1 << 30)
    return np.cumsum(np.array([max(1, weight // spread) for weight in loads]))


def ranked(own_key, dims, number_of, lean):
    table = rank_table(number_of, lean)
    ticket = jax.random.randint(jax.random.fold_in(own_key, 1), dims, 0, int(table[number_of - 1]))
    rank = jnp.searchsorted(jnp.asarray(table, jnp.int32), ticket, side="right")
    return jax.random.permutation(jax.random.fold_in(own_key, 2), number_of)[rank].astype(jnp.int32)


def gaussian(own_key, dims, scale, most, cuts=(), held_as=jnp.bfloat16):
    values = jax.random.normal(own_key, dims, jnp.float32) * scale
    if len(cuts) > 0:
        values = level_of(own_key, dims, cuts, -0.22, 0.18) * values
    return jnp.clip(values, min=-most, max=most).astype(held_as)


def setup_inputs(seed: int = 0) -> dict:
    streams_of = jax.random.split(jax.random.key(seed), 12)
    return {
        "features": gaussian(streams_of[0], (NODES, D), 1.0, 6.0, ((0, 256),)),
        "w_self": gaussian(streams_of[1], (D, OUT), D ** -0.5, 0.375),
        "w_neigh": gaussian(streams_of[2], (D, OUT), (D // 16) ** -0.5, 1.5),
        "bias": gaussian(streams_of[3], (OUT,), 0.5, 3.0, (), jnp.float32),
        "hub_ids": plant(ranked(streams_of[4], (SECTIONS,), N_ROW, 2), jax.random.fold_in(streams_of[4], 3), 0, N_ROW - 1).astype(jnp.int32),
        "hub_adj": draw_hub_adj(jax.random.fold_in(streams_of[11], 71), 0),
        "send_tile": plant(jax.random.randint(streams_of[6], (BLOCKS, N_COL, CAP), 0, NODE_DEV // TILE), jax.random.fold_in(streams_of[6], 1), 0, (NODE_DEV // TILE) - 1).astype(jnp.int32),
        "recv_count": draw_recv_count(jax.random.fold_in(streams_of[11], 71), 0),
        "recv_dst": plant(jax.random.randint(streams_of[8], (BLOCKS, N_COL, CAP), 0, NODE_DEV // TILE), jax.random.fold_in(streams_of[8], 1), 0, (NODE_DEV // TILE) - 1).astype(jnp.int32),
        "recv_adj": draw_recv_adj(jax.random.fold_in(streams_of[11], 71), 0),
        "cotangent": gaussian(streams_of[10], (NODES, OUT), 1.0, 6.0, ((0, 256),)),
    }


def device_pass(feats, hadj, blocks, recv, count, dst, adj, cot, w_self, w_neigh, bias):
    f32 = jnp.float32
    nodes = feats.shape[0]
    width = feats.shape[1]
    peers, slots, tile = adj.shape[0], adj.shape[1], adj.shape[2]
    total = peers * slots
    count_tiles = nodes // tile
    live = (jnp.arange(slots, dtype=jnp.int32)[None, :] < count[:, None]).astype(f32).reshape(total)
    select = (dst.reshape(total)[:, None] == jnp.arange(count_tiles, dtype=jnp.int32)[None, :]).astype(f32) * live[:, None]
    adjs = adj.reshape(total, tile, tile).astype(f32)
    rec = recv.reshape(total, tile, width).astype(f32)
    contrib = jnp.einsum('sij,sjd->sid', adjs, rec)
    tile_sum = jnp.einsum('sn,sid->nid', select, contrib, precision=lax.Precision.HIGHEST).reshape(nodes, width)
    hadj_f = hadj.astype(f32)
    hub_sum = jnp.einsum('snh,shd->nd', hadj_f, blocks.astype(f32))
    tile_deg = jnp.einsum('sn,si->ni', select, jnp.sum(adjs, axis=2), precision=lax.Precision.HIGHEST).reshape(nodes)
    deg = 1.0 + jnp.sum(hadj_f, axis=(0, 2)) + tile_deg
    agg = ((tile_sum + hub_sum) / deg[:, None]).astype(jnp.bfloat16)
    pre = jnp.dot(feats, w_self, preferred_element_type=f32) + jnp.dot(agg, w_neigh, preferred_element_type=f32) + bias
    sig = jax.nn.sigmoid(pre)
    out = (pre * sig).astype(jnp.bfloat16)
    grad = (cot.astype(f32) * sig * (1.0 + pre * (1.0 - sig))).astype(jnp.bfloat16)
    self_grad = jnp.dot(grad, w_self.T, preferred_element_type=f32)
    agg_grad = (jnp.dot(grad, w_neigh.T, preferred_element_type=f32) / deg[:, None]).astype(jnp.bfloat16)
    hub_grad = jnp.einsum('snh,nd->shd', hadj_f, agg_grad.astype(f32))
    rows = agg_grad.reshape(count_tiles, tile, width)[dst.reshape(total)]
    slot_grad = (jnp.einsum('sij,sid->sjd', adjs, rows.astype(f32)) * live[:, None, None]).astype(jnp.bfloat16)
    return out, self_grad, hub_grad, slot_grad.reshape(peers, slots, tile, width)


def reference(features, w_self, w_neigh, bias, hub_ids, hub_adj, send_tile, recv_count, recv_dst, recv_adj, cotangent):
    f32 = jnp.float32
    grid = features.reshape(N_ROW, N_COL, NODE_DEV, D)
    hubs = grid[hub_ids][:, :, :HUB]
    hub_cols = jnp.transpose(hubs, (1, 0, 2, 3))
    count_tiles = NODE_DEV // TILE
    cot_blocks = cotangent.reshape(N_ROW * N_COL, NODE_DEV, OUT)
    columns = jnp.arange(N_COL, dtype=jnp.int32)

    def one_row(carry, row):
        start = (row * N_COL).astype(jnp.int32)
        rows_x = lax.dynamic_index_in_dim(grid, row, 0, keepdims=False)

        def take(array):
            return lax.dynamic_slice_in_dim(array, start, N_COL, 0)

        hadj = take(hub_adj)
        stile = take(send_tile)
        rcount = take(recv_count)
        rdst = take(recv_dst)
        radj = take(recv_adj)
        cot_rows = take(cot_blocks)
        tiles = rows_x.reshape(N_COL, count_tiles, TILE, D)
        picked = jnp.transpose(stile, (1, 0, 2))
        received = tiles[columns[None, :, None], picked]
        out, self_grad, hub_grad, slot_grad = jax.vmap(
            device_pass, in_axes=(0, 0, 0, 0, 0, 0, 0, 0, None, None, None))(
            rows_x, hadj, hub_cols, received, rcount, rdst, radj, cot_rows, w_self, w_neigh, bias)
        select = (stile[..., None] == jnp.arange(count_tiles, dtype=jnp.int32)).astype(f32)
        returned = jnp.einsum('pckn,cpkid->pnid', select, slot_grad.astype(f32),
                              precision=lax.Precision.HIGHEST).reshape(N_COL, NODE_DEV, D)
        return carry + hub_grad, (out, self_grad + returned)

    start_carry = jnp.zeros((N_COL, SECTIONS, HUB, D), f32)
    hub_total, (outs, grads) = lax.scan(one_row, start_carry, jnp.arange(N_ROW, dtype=jnp.int32))
    for section in range(SECTIONS):
        grads = grads.at[hub_ids[section], :, :HUB].add(hub_total[:, section])
    return outs.reshape(NODES, OUT), grads.reshape(NODES, D).astype(jnp.bfloat16)
```

```python
import jax
import jax.numpy as jnp
from jax import lax
from jax.sharding import PartitionSpec as P


def shards(
    features,
    w_self,
    w_neigh,
    bias,
    hub_ids,
    hub_adj,
    send_tile,
    recv_count,
    recv_dst,
    recv_adj,
    cotangent,
):
    f32 = jnp.float32
    bf16 = jnp.bfloat16
    nodes, width = features.shape
    sections = hub_ids.shape[0]
    hub_rows = hub_adj.shape[3]
    peers, slots, tile = (recv_adj.shape[1], recv_adj.shape[2], recv_adj.shape[3])
    total = peers * slots
    count_tiles = nodes // tile
    adjacency = hub_adj[0]
    rows_n = lax.axis_size("row")
    part = hub_rows // rows_n
    pieces = lax.all_to_all(
        features[:hub_rows].reshape(rows_n, part, width), "row", split_axis=0, concat_axis=0, tiled=True
    )
    picked = jnp.stack(
        [lax.dynamic_index_in_dim(pieces, hub_ids[s], 0, keepdims=False) for s in range(sections)]
    )
    gathered = lax.all_gather(picked, "row", axis=0, tiled=False)
    blocks = jnp.transpose(gathered, (1, 0, 2, 3)).reshape(sections, hub_rows, width)
    hub_sum = jnp.zeros((nodes, width), f32)
    for section in range(sections):
        hub_sum = hub_sum + jnp.dot(adjacency[section], blocks[section], preferred_element_type=f32)
    offered = send_tile[0].reshape(total)
    outgoing = jnp.stack(
        [lax.dynamic_slice_in_dim(features, offered[i] * tile, tile, 0) for i in range(total)]
    ).reshape(peers, slots, tile, width)
    incoming = lax.all_to_all(outgoing, "col", split_axis=0, concat_axis=0, tiled=True)
    live = (
        (jnp.arange(slots, dtype=jnp.int32)[None, :] < recv_count[0][:, None])
        .astype(f32)
        .reshape(total)
    )
    landing = recv_dst[0].reshape(total)
    select = (landing[:, None] == jnp.arange(count_tiles, dtype=jnp.int32)[None, :]).astype(
        f32
    ) * live[:, None]
    weights = recv_adj[0].reshape(total, tile, tile)
    contrib = jnp.einsum(
        "sij,sjd->sid", weights, incoming.reshape(total, tile, width), preferred_element_type=f32
    )
    tile_sum = jnp.einsum("sn,sid->nid", select, contrib, precision=lax.Precision.HIGHEST).reshape(
        nodes, width
    )
    row_weight = jnp.sum(weights.astype(f32), axis=2)
    tile_deg = jnp.einsum("sn,si->ni", select, row_weight, precision=lax.Precision.HIGHEST).reshape(
        nodes
    )
    degree = 1.0 + jnp.sum(adjacency.astype(f32), axis=(0, 2)) + tile_deg
    agg = ((tile_sum + hub_sum) / degree[:, None]).astype(bf16)
    pre = (
        jnp.dot(features, w_self, preferred_element_type=f32)
        + jnp.dot(agg, w_neigh, preferred_element_type=f32)
        + bias
    )
    sig = jax.nn.sigmoid(pre)
    output = (pre * sig).astype(bf16)
    grad = (cotangent.astype(f32) * sig * (1.0 + pre * (1.0 - sig))).astype(bf16)
    contract = (((1,), (1,)), ((), ()))
    self_grad = lax.dot_general(grad, w_self, contract, preferred_element_type=f32)
    agg_grad = (
        lax.dot_general(grad, w_neigh, contract, preferred_element_type=f32) / degree[:, None]
    ).astype(bf16)
    partials = jnp.stack(
        [
            lax.dot_general(
                adjacency[section], agg_grad, (((0,), (0,)), ((), ())), preferred_element_type=f32
            ).astype(bf16)
            for section in range(sections)
        ]
    ).reshape(sections, rows_n, part, width)
    landed = lax.all_to_all(partials, "row", split_axis=1, concat_axis=1, tiled=True)
    summed = jnp.sum(landed.astype(f32), axis=1)
    owners = (hub_ids[None, :] == jnp.arange(rows_n, dtype=jnp.int32)[:, None]).astype(f32)
    to_owner = jnp.sum(owners[:, :, None, None] * summed[None], axis=1).astype(bf16)
    hub_back = (
        lax.all_to_all(to_owner, "row", split_axis=0, concat_axis=0, tiled=True)
        .astype(f32)
        .reshape(hub_rows, width)
    )
    dest_rows = jnp.stack(
        [lax.dynamic_slice_in_dim(agg_grad, landing[i] * tile, tile, 0) for i in range(total)]
    )
    slot_grad = (
        jnp.einsum("sij,sid->sjd", weights, dest_rows, preferred_element_type=f32)
        * live[:, None, None]
    ).astype(bf16)
    returned = lax.all_to_all(
        slot_grad.reshape(peers, slots, tile, width), "col", split_axis=0, concat_axis=0, tiled=True
    )
    owned = (offered[:, None] == jnp.arange(count_tiles, dtype=jnp.int32)[None, :]).astype(f32)
    tile_back = jnp.einsum(
        "sn,sid->nid",
        owned,
        returned.reshape(total, tile, width).astype(f32),
        precision=lax.Precision.HIGHEST,
    ).reshape(nodes, width)
    hub_padded = jnp.concatenate([hub_back, jnp.zeros((nodes - hub_rows, width), f32)], axis=0)
    feature_grad = (self_grad + tile_back + hub_padded).astype(bf16)
    return (output, feature_grad)


def solution(mesh):
    placed = (
        P(("row", "col"), None),
        P(),
        P(),
        P(),
        P(),
        P(("row", "col"), None, None, None),
        P(("row", "col"), None, None),
        P(("row", "col"), None),
        P(("row", "col"), None, None),
        P(("row", "col"), None, None, None, None),
        P(("row", "col"), None),
    )
    return jax.shard_map(
        shards,
        mesh=mesh,
        in_specs=placed,
        out_specs=(P(("row", "col"), None), P(("row", "col"), None)),
        check_vma=False,
    )
```

```python
import functools

import jax
import jax.numpy as jnp
from jax import lax
from jax.experimental import pallas as pl
from jax.experimental.pallas import tpu as pltpu
from jax.sharding import PartitionSpec as P

MESH = pl.DeviceIdType.MESH
F32 = jnp.float32
BF16 = jnp.bfloat16
CHUNK = 512
NT = (((1,), (1,)), ((), ()))


def offsets(n):
    return sorted(range(1, n), key=lambda d: min(d, n - d))


def dot(a, b):
    return jnp.dot(a, b, preferred_element_type=F32)


def layer_kernel(
    n_row,
    n_col,
    send_ref,
    count_ref,
    dest_ref,
    hub_ref,
    ws,
    wn,
    bias,
    feat_hbm,
    hadj_hbm,
    radj_hbm,
    cot_hbm,
    out_hbm,
    fg_hbm,
    fv,
    hv,
    av,
    avt,
    cv,
    ov,
    gv,
    agv,
    agt,
    fgv,
    pre,
    hs,
    rd,
    outb,
    inc,
    retb,
    rin,
    relf,
    relb,
    chain,
    dchain,
    back,
    a_in,
    b_in,
    sel,
    hb,
    ps,
    sb,
    rs,
    rl,
    ow,
    osib,
    bk,
    bl,
    landed,
    prev_f,
    last_f,
    owned,
    prev_b,
    last_b,
    loc_sem,
    zf_s,
    zf_r,
    zb_s,
    zb_r,
    rf_s,
    rf_r,
    rb_s,
    rb_r,
    a_s,
    a_r,
    g_s,
    g_r,
    c_s,
    c_r,
    d_s,
    d_r,
    sib_s,
    sib_r,
):
    row = lax.axis_index("row")
    col = lax.axis_index("col")
    chip = row // 2
    core = lax.rem(row, 2)
    sib = chip * 2 + 1 - core
    chips = n_row // 2
    nodes, width = ov.shape
    sections, hub_rows = hv.shape[0], hv.shape[2]
    slots, tile = av.shape[1], av.shape[2]
    tiles = nodes // tile
    part = hub_rows // chips
    half = width // 2
    order = offsets(n_col)
    opposite = n_col // 2
    step = opposite // 2
    ways = (step, n_col - step)
    total = slots * n_col
    chunks = nodes // CHUNK
    per = CHUNK // tile
    mine = pl.ds(pl.multiple_of(core * half, half), half)
    other = pl.ds(pl.multiple_of((1 - core) * half, half), half)
    own_part = pl.ds(pl.multiple_of(chip * part, part), part)

    def tile_rows(t):
        return pl.ds(pl.multiple_of(t * tile, tile), tile)

    def chunk_rows(c):
        return pl.ds(pl.multiple_of(c * CHUNK, CHUNK), CHUNK)

    def tiles_of(ref, c):
        return jnp.concatenate([ref[c * per + t] for t in range(per)], axis=0)

    def loop(n, body, start=0):
        def run(i, carry):
            body(i)
            return carry

        lax.fori_loop(start, n, run, 0)

    def remote(src, dst, send, recv, to):
        return pltpu.make_async_remote_copy(
            src_ref=src, dst_ref=dst, send_sem=send, recv_sem=recv, device_id=to, device_id_type=MESH
        )

    def to_col(d):
        return (row, lax.rem(col + d, n_col))

    def chip_of(d):
        return lax.rem(chip + d, chips)

    def to_chip(d):
        return (chip_of(d) * 2 + core, col)

    def part_of(j):
        return pl.ds(pl.multiple_of(j * part, part), part)

    barrier = pltpu.get_barrier_semaphore()
    for d in order:
        pl.semaphore_signal(barrier, inc=1, device_id=to_col(d), device_id_type=MESH)

    def greet(d):
        pl.semaphore_signal(barrier, inc=1, device_id=to_chip(d), device_id_type=MESH)

    loop(chips, greet, 1)
    pl.semaphore_signal(barrier, inc=1, device_id=(sib, col), device_id_type=MESH)

    load_f = pltpu.make_async_copy(feat_hbm, fv, loc_sem.at[0])
    load_a = pltpu.make_async_copy(radj_hbm, av, loc_sem.at[1])
    load_h = pltpu.make_async_copy(hadj_hbm, hv, loc_sem.at[2])
    load_c = pltpu.make_async_copy(cot_hbm, cv, loc_sem.at[3])
    load_f.start()
    load_a.start()
    load_h.start()
    load_c.start()
    load_f.wait()

    def stage(i, d):
        to = lax.rem(col + d, n_col)
        for k in range(slots):
            outb[i, k] = fv[send_ref[to * slots + k]]

    stage(0, order[0])
    stage(len(order) - 1, order[-1])
    pl.semaphore_wait(barrier, n_col - 1 + chips - 1 + 1)

    def ring(buf, land, send, recv, sign):
        copies = {}
        for i, d in enumerate(order):
            to = d if sign > 0 else n_col - d
            if d != opposite:
                copies[i] = remote(buf.at[i], land.at[i], send.at[i, 0], recv.at[i, 0], to_col(to))
        return copies

    def relay_first(buf, rel, send, recv):
        i = len(order) - 1
        return [
            remote(buf.at[i, k], rel.at[k], send.at[k], recv.at[k], to_col(ways[k]))
            for k in range(slots)
        ]

    def relay_second(rel, land, send, recv):
        i = len(order) - 1
        return [
            remote(rel.at[k], land.at[i, k], send.at[i, k], recv.at[i, k], to_col(ways[k]))
            for k in range(slots)
        ]

    fwd = ring(outb, inc, zf_s, zf_r, 1)
    fwd1 = relay_first(outb, relf, rf_s, rf_r)
    fwd2 = relay_second(relf, inc, zf_s, zf_r)
    for c in fwd1:
        c.start()
    fwd[0].start()

    per_tile = tile // part

    def hub_of(j):
        return fv.at[j // per_tile, part_of(lax.rem(j, per_tile)), :]

    def hub_a(d):
        return remote(hub_of(chip_of(d)), a_in.at[chip], a_s.at[d], a_r.at[d], to_chip(d))

    loop(chips, lambda d: hub_a(d).start(), 1)
    a_in[chip] = fv[chip // per_tile, part_of(lax.rem(chip, per_tile)), :]
    for i in range(1, len(order) - 1):
        stage(i, order[i])
        fwd[i].start()

    def self_part(c):
        rows = chunk_rows(c)
        pre[rows, :] = dot(tiles_of(fv, c), ws[...]) + bias[...]

    loop(chunks, self_part)

    loop(chips, lambda d: hub_a(d).wait_recv(), 1)
    swap_b = remote(a_in.at[:, :, other], b_in, sib_s.at[0], sib_r.at[0], (sib, col))
    swap_b.start()

    def source(s):
        d = ([0] + order)[s // slots]
        return lax.rem(col + n_col - d, n_col) * slots + s % slots

    def target(s):
        d = ([0] + order)[s // slots]
        return lax.rem(col + d, n_col) * slots + s % slots

    def is_live(s):
        d = ([0] + order)[s // slots]
        return (s % slots) < count_ref[lax.rem(col + n_col - d, n_col)]

    for s in range(total):
        landed[s] = jnp.where(is_live(s), dest_ref[source(s)], -1)
        owned[s] = send_ref[target(s)]

    def link(keys, prev, last):
        def before(s):
            key = keys[s]
            found = total
            for t in range(total):
                found = jnp.where((t < s) & (keys[t] == key), t, found)
            prev[s] = found

        def final(n):
            found = total
            for t in range(total):
                found = jnp.where(keys[t] == n, t, found)
            last[n] = found

        loop(total, before)
        loop(tiles, final)

    link(landed, prev_f, last_f)
    link(owned, prev_b, last_b)
    chain[total] = jnp.zeros((tile, width), F32)
    back[total] = jnp.zeros((tile, width), F32)
    dchain[total] = jnp.zeros((tile, tile), F32)

    swap_b.wait_recv()
    for s in range(sections):
        h = hub_ref[s]
        h_chip = h // 2
        h_core = h - 2 * h_chip
        both = a_in[h_chip].astype(F32)
        same = jnp.where(core == 0, both[:, :half], both[:, half:])
        across = b_in[h_chip].astype(F32)
        sel[s] = jnp.where(h_core == core, same, across).astype(BF16)
    spread = hb.at[:, own_part, mine]

    def hub_g(d):
        return remote(sel, spread, g_s.at[d], g_r.at[d], to_chip(d))

    loop(chips, lambda d: hub_g(d).start(), 1)
    for s in range(sections):
        hb[s, own_part, mine] = sel[s]

    load_a.wait()
    ones_t = jnp.ones((tile, tile), BF16)

    def weights(s):
        d = ([0] + order)[s // slots]
        return lax.rem(col + n_col - d, n_col), s % slots

    for s in range(total):
        p, k = weights(s)
        w = av[p, k]
        dchain[s] = dot(w, ones_t) + dchain[prev_f[s]]
        avt[s] = w.astype(F32).T.astype(BF16)

    for c in range(slots):
        fwd1[c].wait_recv()
        fwd2[c].start()

    load_h.wait()
    ones_h = jnp.ones((hub_rows, half), BF16)

    def degrees(c):
        rows = chunk_rows(c)
        deg = 1.0 + jnp.concatenate([dchain[last_f[c * per + t]] for t in range(per)], axis=0)
        for s in range(sections):
            deg = deg + dot(hv[s, rows, :], ones_h)
        rd[rows, :] = 1.0 / deg

    loop(chunks, degrees)

    loop(chips, lambda d: hub_g(d).wait_recv(), 1)
    swap_h = remote(hb.at[:, :, mine], hb.at[:, :, mine], sib_s.at[1], sib_r.at[1], (sib, col))
    swap_h.start()
    swap_h.wait_recv()

    def hub_sum(c):
        rows = chunk_rows(c)
        acc = dot(hv[0, rows, :], hb[0])
        for s in range(1, sections):
            acc = acc + dot(hv[s, rows, :], hb[s])
        hs[rows, :] = acc

    loop(chunks, hub_sum)

    for s in range(total):
        i, k = s // slots - 1, s % slots
        p, _ = weights(s)
        if i < 0:
            arrived = fv[send_ref[target(s)]]
        else:
            if order[i] == opposite:
                fwd2[k].wait_recv()
            elif k == 0:
                fwd[i].wait_recv()
            arrived = inc[i, k]
        chain[s] = dot(av[p, k], arrived) + chain[prev_f[s]]
    load_c.wait()

    def middle(c):
        rows = chunk_rows(c)
        raw = hs[rows, :] + jnp.concatenate(
            [chain[last_f[c * per + t]] for t in range(per)], axis=0
        )
        inv = jnp.concatenate([rd[rows, :]] * (width // half), axis=1)
        agg = (raw * inv).astype(BF16)
        x = pre[rows, :] + dot(agg, wn[...])
        sig = 0.5 * jnp.tanh(0.5 * x) + 0.5
        ov[rows, :] = (x * sig).astype(BF16)
        grad = (cv[rows, :].astype(F32) * sig * (1.0 + x * (1.0 - sig))).astype(BF16)
        gv[rows, :] = grad
        back_grad = lax.dot_general(grad, wn[...], NT, preferred_element_type=F32)
        scaled = (back_grad * inv).astype(BF16)
        for t in range(per):
            agv[c * per + t] = scaled[t * tile : (t + 1) * tile]

    loop(chunks, middle)

    def slot_grad(s):
        rows = agv[dest_ref[source(s)]]
        value = jnp.where(is_live(s), dot(avt[s], rows), 0.0)
        return value.astype(BF16)

    bwd = ring(retb, rin, zb_s, zb_r, -1)
    bwd1 = relay_first(retb, relb, rb_s, rb_r)
    bwd2 = relay_second(relb, rin, zb_s, zb_r)
    for i in [len(order) - 1] + list(range(len(order) - 1)):
        for k in range(slots):
            retb[i, k] = slot_grad((i + 1) * slots + k)
        if order[i] == opposite:
            for c in bwd1:
                c.start()
        else:
            bwd[i].start()
    for k in range(slots):
        back[k] = slot_grad(k).astype(F32) + back[prev_b[k]]

    store_o = pltpu.make_async_copy(ov, out_hbm, loc_sem.at[4])
    store_o.start()

    def turn(c):
        agt[:, chunk_rows(c)] = tiles_of(agv, c).astype(F32).T.astype(BF16)

    loop(chunks, turn)

    def hub_part(s):
        value = dot(agt[...], hv[s])
        ps[0, s] = value[:, :half]
        ps[1, s] = value[:, half:]

    loop(sections, hub_part)
    swap_p = remote(ps.at[1 - core], sb, sib_s.at[2], sib_r.at[2], (sib, col))
    swap_p.start()

    def self_grad(c):
        rows = chunk_rows(c)
        pre[rows, :] = lax.dot_general(gv[rows, :], ws[...], NT, preferred_element_type=F32)

    loop(chunks, self_grad)
    swap_p.wait_recv()

    def pair(s):
        rs[s] = (ps[core, s] + sb[s]).astype(BF16)

    loop(sections, pair)

    def hub_c(d):
        return remote(rs.at[:, part_of(chip_of(d)), :], rl.at[chip], c_s.at[d], c_r.at[d], to_chip(d))

    loop(chips, lambda d: hub_c(d).start(), 1)
    for s in range(sections):
        rl[chip, s] = rs[s, own_part, :]
    for c in range(slots):
        bwd1[c].wait_recv()
        bwd2[c].start()
    loop(chips, lambda d: hub_c(d).wait_recv(), 1)
    tot = [rl[0, s].astype(F32) for s in range(sections)]
    for j in range(1, chips):
        tot = [tot[s] + rl[j, s].astype(F32) for s in range(sections)]

    def owners(j):
        for b in range(2):
            value = jnp.zeros((part, half), F32)
            for s in range(sections):
                value = value + jnp.where(hub_ref[s] == j * 2 + b, tot[s], 0.0)
            ow[b, j] = value

    loop(chips, owners)
    swap_o = remote(ow.at[1 - core], osib, sib_s.at[3], sib_r.at[3], (sib, col))
    swap_o.start()
    swap_o.wait_recv()

    def owner_rows(j):
        same = ow[core, j]
        across = osib[j]
        bk[j] = jnp.concatenate(
            [jnp.where(core == 0, same, across), jnp.where(core == 0, across, same)], axis=1
        )

    loop(chips, owner_rows)

    def hub_d(d):
        return remote(bk.at[chip_of(d)], bl.at[own_part, :], d_s.at[d], d_r.at[d], to_chip(d))

    loop(chips, lambda d: hub_d(d).start(), 1)
    bl[own_part, :] = bk[chip]
    loop(chips, lambda d: hub_d(d).wait_recv(), 1)
    pre[pl.ds(0, hub_rows), :] += bl[...].T

    for s in range(slots, total):
        i, k = s // slots - 1, s % slots
        if order[i] == opposite:
            bwd2[k].wait_recv()
        elif k == 0:
            bwd[i].wait_recv()
        back[s] = rin[i, k].astype(F32) + back[prev_b[s]]

    def finish(n):
        rows = tile_rows(n)
        fgv[rows, :] = (pre[rows, :] + back[last_b[n]]).astype(BF16)

    loop(tiles, finish)
    store_g = pltpu.make_async_copy(fgv, fg_hbm, loc_sem.at[5])
    store_g.start()

    for c in list(fwd.values()) + fwd1 + fwd2 + list(bwd.values()) + bwd1 + bwd2:
        c.wait_send()
    for c in (swap_b, swap_h, swap_p, swap_o):
        c.wait_send()
    loop(chips, lambda d: hub_a(d).wait_send(), 1)
    loop(chips, lambda d: hub_g(d).wait_send(), 1)
    loop(chips, lambda d: hub_c(d).wait_send(), 1)
    loop(chips, lambda d: hub_d(d).wait_send(), 1)
    store_o.wait()
    store_g.wait()


def shards(
    features,
    w_self,
    w_neigh,
    bias,
    hub_ids,
    hub_adj,
    send_tile,
    recv_count,
    recv_dst,
    recv_adj,
    cotangent,
):
    n_row, n_col = lax.axis_size("row"), lax.axis_size("col")
    nodes, width = features.shape
    sections, hub_rows = hub_adj.shape[1], hub_adj.shape[3]
    peers, slots, tile = recv_adj.shape[1:4]
    total = peers * slots
    tiles = nodes // tile
    chips = n_row // 2
    part = hub_rows // chips
    half = width // 2
    others = n_col - 1
    vmem, smem, dma = pltpu.VMEM, pltpu.SMEM, pltpu.SemaphoreType.DMA
    spec = lambda space: pl.BlockSpec(memory_space=space)
    return pl.pallas_call(
        functools.partial(layer_kernel, n_row, n_col),
        out_shape=(
            jax.ShapeDtypeStruct((nodes, width), BF16),
            jax.ShapeDtypeStruct((nodes, width), BF16),
        ),
        in_specs=[spec(smem)] * 4 + [spec(vmem)] * 3 + [spec(pl.ANY)] * 4,
        out_specs=(spec(pl.ANY), spec(pl.ANY)),
        scratch_shapes=[
            vmem((tiles, tile, width), BF16),
            vmem((sections, nodes, hub_rows), BF16),
            vmem((peers, slots, tile, tile), BF16),
            vmem((total, tile, tile), BF16),
            vmem((nodes, width), BF16),
            vmem((nodes, width), BF16),
            vmem((nodes, width), BF16),
            vmem((tiles, tile, width), BF16),
            vmem((width, nodes), BF16),
            vmem((nodes, width), BF16),
            vmem((nodes, width), F32),
            vmem((nodes, width), F32),
            vmem((nodes, half), F32),
            vmem((others, slots, tile, width), BF16),
            vmem((others, slots, tile, width), BF16),
            vmem((others, slots, tile, width), BF16),
            vmem((others, slots, tile, width), BF16),
            vmem((slots, tile, width), BF16),
            vmem((slots, tile, width), BF16),
            vmem((total + 1, tile, width), F32),
            vmem((total + 1, tile, tile), F32),
            vmem((total + 1, tile, width), F32),
            vmem((chips, part, width), BF16),
            vmem((chips, part, half), BF16),
            vmem((sections, part, half), BF16),
            vmem((sections, hub_rows, width), BF16),
            vmem((2, sections, width, half), F32),
            vmem((sections, width, half), F32),
            vmem((sections, width, half), BF16),
            vmem((chips, sections, part, half), BF16),
            vmem((2, chips, part, half), F32),
            vmem((chips, part, half), F32),
            vmem((chips, part, width), F32),
            vmem((hub_rows, width), F32),
            smem((total,), jnp.int32),
            smem((total,), jnp.int32),
            smem((tiles,), jnp.int32),
            smem((total,), jnp.int32),
            smem((total,), jnp.int32),
            smem((tiles,), jnp.int32),
            dma((6,)),
            dma((others, slots)),
            dma((others, slots)),
            dma((others, slots)),
            dma((others, slots)),
            dma((slots,)),
            dma((slots,)),
            dma((slots,)),
            dma((slots,)),
            dma((chips,)),
            dma((chips,)),
            dma((chips,)),
            dma((chips,)),
            dma((chips,)),
            dma((chips,)),
            dma((chips,)),
            dma((chips,)),
            dma((4,)),
            dma((4,)),
        ],
        compiler_params=pltpu.CompilerParams(
            collective_id=0, has_side_effects=True, vmem_limit_bytes=52 * 2**20
        ),
        name="layer",
    )(
        send_tile.reshape(total),
        recv_count.reshape(peers),
        recv_dst.reshape(total),
        hub_ids,
        w_self,
        w_neigh,
        bias.reshape(1, width),
        features.reshape(tiles, tile, width),
        hub_adj.reshape(hub_adj.shape[1:]),
        recv_adj.reshape(recv_adj.shape[1:]),
        cotangent,
    )


def solution(mesh):
    placed = (
        P(("row", "col"), None),
        P(),
        P(),
        P(),
        P(),
        P(("row", "col"), None, None, None),
        P(("row", "col"), None, None),
        P(("row", "col"), None),
        P(("row", "col"), None, None),
        P(("row", "col"), None, None, None, None),
        P(("row", "col"), None),
    )
    return jax.shard_map(
        shards,
        mesh=mesh,
        in_specs=placed,
        out_specs=(P(("row", "col"), None), P(("row", "col"), None)),
        check_vma=False,
    )
```

```python
import functools

import jax
import jax.numpy as jnp
from jax import lax
from jax.experimental import pallas as pl
from jax.experimental.pallas import tpu as pltpu
from jax.sharding import PartitionSpec as P

MESH = pl.DeviceIdType.MESH
F32 = jnp.float32
BF16 = jnp.bfloat16
CHUNK = 512
PIECES = 4
NT = (((1,), (1,)), ((), ()))


def offsets(n):
    return sorted(range(1, n), key=lambda d: min(d, n - d))


def dot(a, b):
    return jnp.dot(a, b, preferred_element_type=F32)


def layer_kernel(
    n_row,
    n_col,
    send_hbm,
    count_hbm,
    dest_hbm,
    hub_hbm,
    ws_hbm,
    wn_hbm,
    bias_hbm,
    feat_hbm,
    hadj_hbm,
    radj_hbm,
    cot_hbm,
    out_hbm,
    fg_hbm,
    send_ref,
    count_ref,
    dest_ref,
    hub_ref,
    ws,
    wn,
    bias,
    fv,
    hv,
    av,
    avt,
    cv,
    ov,
    gv,
    agv,
    agt,
    fgv,
    pre,
    hs,
    rd,
    outb,
    inc,
    retb,
    rin,
    chain,
    dchain,
    back,
    a_in,
    b_in,
    sel,
    hb,
    ps,
    sb,
    rs,
    rl,
    ow,
    osib,
    bk,
    bl,
    landed,
    prev_f,
    last_f,
    owned,
    prev_b,
    last_b,
    loc_sem,
    zf_s,
    zf_r,
    zb_s,
    zb_r,
    a_s,
    a_r,
    g_s,
    g_r,
    c_s,
    c_r,
    d_s,
    d_r,
    sib_s,
    sib_r,
):
    row = lax.axis_index("row")
    col = lax.axis_index("col")
    chip = row // 2
    core = lax.rem(row, 2)
    sib = chip * 2 + 1 - core
    chips = n_row // 2
    nodes, width = ov.shape
    sections, hub_rows = hv.shape[0], hv.shape[2]
    slots, tile = av.shape[1], av.shape[2]
    tiles = nodes // tile
    part = hub_rows // chips
    half = width // 2
    order = offsets(n_col)
    total = slots * n_col
    chunks = nodes // CHUNK
    per = CHUNK // tile
    mine = pl.ds(pl.multiple_of(core * half, half), half)
    other = pl.ds(pl.multiple_of((1 - core) * half, half), half)
    own_part = pl.ds(pl.multiple_of(chip * part, part), part)

    def tile_rows(t):
        return pl.ds(pl.multiple_of(t * tile, tile), tile)

    def chunk_rows(c):
        return pl.ds(pl.multiple_of(c * CHUNK, CHUNK), CHUNK)

    def tiles_of(ref, c):
        return jnp.concatenate([ref[c * per + t] for t in range(per)], axis=0)

    def loop(n, body, start=0):
        def run(i, carry):
            body(i)
            return carry

        lax.fori_loop(start, n, run, 0)

    def remote(src, dst, send, recv, to):
        return pltpu.make_async_remote_copy(
            src_ref=src, dst_ref=dst, send_sem=send, recv_sem=recv, device_id=to, device_id_type=MESH
        )

    def to_col(d):
        return (row, lax.rem(col + d, n_col))

    def chip_of(d):
        return lax.rem(chip + d, chips)

    def to_chip(d):
        return (chip_of(d) * 2 + core, col)

    def part_of(j):
        return pl.ds(pl.multiple_of(j * part, part), part)

    barrier = pltpu.get_barrier_semaphore()
    for d in order:
        pl.semaphore_signal(barrier, inc=1, device_id=to_col(d), device_id_type=MESH)

    def greet(d):
        pl.semaphore_signal(barrier, inc=1, device_id=to_chip(d), device_id_type=MESH)

    loop(chips, greet, 1)
    pl.semaphore_signal(barrier, inc=1, device_id=(sib, col), device_id_type=MESH)

    pairs = (
        (send_hbm, send_ref),
        (feat_hbm, fv),
        (dest_hbm, dest_ref),
        (count_hbm, count_ref),
        (hub_hbm, hub_ref),
        (ws_hbm, ws),
        (bias_hbm, bias),
        (radj_hbm, av),
        (hadj_hbm, hv),
        (wn_hbm, wn),
        (cot_hbm, cv),
    )
    loads = [pltpu.make_async_copy(src, dst, loc_sem.at[i]) for i, (src, dst) in enumerate(pairs)]
    for c in loads:
        c.start()
    loads[0].wait()
    loads[1].wait()

    def stage(i, d):
        to = lax.rem(col + d, n_col)
        for k in range(slots):
            outb[i, k] = fv[send_ref[k, to]]

    stage(0, order[0])
    pl.semaphore_wait(barrier, n_col - 1 + chips - 1 + 1)

    def ring(buf, land, send, recv, sign):
        return [
            remote(buf.at[i], land.at[i], send.at[i], recv.at[i], to_col(d if sign > 0 else n_col - d))
            for i, d in enumerate(order)
        ]

    fwd = ring(outb, inc, zf_s, zf_r, 1)
    fwd[0].start()

    per_tile = tile // part

    def hub_of(j):
        return fv.at[j // per_tile, part_of(lax.rem(j, per_tile)), :]

    def hub_a(d):
        return remote(hub_of(chip_of(d)), a_in.at[chip], a_s.at[d], a_r.at[d], to_chip(d))

    loop(chips, lambda d: hub_a(d).start(), 1)
    a_in[chip] = fv[chip // per_tile, part_of(lax.rem(chip, per_tile)), :]
    for i in range(1, len(order)):
        stage(i, order[i])
        fwd[i].start()

    loads[5].wait()
    loads[6].wait()

    def self_part(c):
        rows = chunk_rows(c)
        pre[rows, :] = dot(tiles_of(fv, c), ws[...]) + bias[...]

    loop(chunks, self_part)

    loop(chips, lambda d: hub_a(d).wait_recv(), 1)
    swap_b = remote(a_in.at[:, :, other], b_in, sib_s.at[0], sib_r.at[0], (sib, col))
    swap_b.start()

    for c in loads[2:5]:
        c.wait()

    def offset(s):
        return ([0] + order)[s // slots]

    def weights(s):
        return lax.rem(col + n_col - offset(s), n_col), s % slots

    def landing(s):
        p, k = weights(s)
        return dest_ref[k, p]

    def offered(s):
        return send_ref[s % slots, lax.rem(col + offset(s), n_col)]

    def is_live(s):
        p, k = weights(s)
        return k < count_ref[p]

    for s in range(total):
        landed[s] = jnp.where(is_live(s), landing(s), -1)
        owned[s] = offered(s)

    def link(keys, prev, last):
        def before(s):
            key = keys[s]
            found = total
            for t in range(total):
                found = jnp.where((t < s) & (keys[t] == key), t, found)
            prev[s] = found

        def final(n):
            found = total
            for t in range(total):
                found = jnp.where(keys[t] == n, t, found)
            last[n] = found

        loop(total, before)
        loop(tiles, final)

    link(landed, prev_f, last_f)
    link(owned, prev_b, last_b)
    chain[total] = jnp.zeros((tile, width), F32)
    back[total] = jnp.zeros((tile, width), F32)
    dchain[total] = jnp.zeros((tile, tile), F32)

    swap_b.wait_recv()
    for s in range(sections):
        h = hub_ref[s]
        h_chip = h // 2
        h_core = h - 2 * h_chip
        both = a_in[h_chip].astype(F32)
        same = jnp.where(core == 0, both[:, :half], both[:, half:])
        across = b_in[h_chip].astype(F32)
        sel[s] = jnp.where(h_core == core, same, across).astype(BF16)
    spread = hb.at[:, own_part, mine]

    def hub_g(d):
        return remote(sel, spread, g_s.at[d], g_r.at[d], to_chip(d))

    loop(chips, lambda d: hub_g(d).start(), 1)
    for s in range(sections):
        hb[s, own_part, mine] = sel[s]

    loads[7].wait()
    ones_t = jnp.ones((tile, tile), BF16)

    for s in range(total):
        p, k = weights(s)
        w = av[p, k]
        dchain[s] = dot(w, ones_t) + dchain[prev_f[s]]
        avt[s] = w.astype(F32).T.astype(BF16)

    loads[8].wait()
    ones_h = jnp.ones((hub_rows, half), BF16)

    def degrees(c):
        rows = chunk_rows(c)
        deg = 1.0 + jnp.concatenate([dchain[last_f[c * per + t]] for t in range(per)], axis=0)
        for s in range(sections):
            deg = deg + dot(hv[s, rows, :], ones_h)
        rd[rows, :] = 1.0 / deg

    loop(chunks, degrees)

    loop(chips, lambda d: hub_g(d).wait_recv(), 1)
    swap_h = remote(hb.at[:, :, mine], hb.at[:, :, mine], sib_s.at[1], sib_r.at[1], (sib, col))
    swap_h.start()
    swap_h.wait_recv()

    def hub_sum(c):
        rows = chunk_rows(c)
        acc = dot(hv[0, rows, :], hb[0])
        for s in range(1, sections):
            acc = acc + dot(hv[s, rows, :], hb[s])
        hs[rows, :] = acc

    loop(chunks, hub_sum)

    for s in range(total):
        i, k = s // slots - 1, s % slots
        p, _ = weights(s)
        if i < 0:
            arrived = fv[offered(s)]
        else:
            if k == 0:
                fwd[i].wait_recv()
            arrived = inc[i, k]
        chain[s] = dot(av[p, k], arrived) + chain[prev_f[s]]
    loads[9].wait()
    loads[10].wait()

    def middle(c):
        rows = chunk_rows(c)
        raw = hs[rows, :] + jnp.concatenate(
            [chain[last_f[c * per + t]] for t in range(per)], axis=0
        )
        inv = jnp.concatenate([rd[rows, :]] * (width // half), axis=1)
        agg = (raw * inv).astype(BF16)
        x = pre[rows, :] + dot(agg, wn[...])
        sig = 0.5 * jnp.tanh(0.5 * x) + 0.5
        ov[rows, :] = (x * sig).astype(BF16)
        grad = (cv[rows, :].astype(F32) * sig * (1.0 + x * (1.0 - sig))).astype(BF16)
        gv[rows, :] = grad
        back_grad = lax.dot_general(grad, wn[...], NT, preferred_element_type=F32)
        scaled = (back_grad * inv).astype(BF16)
        for t in range(per):
            agv[c * per + t] = scaled[t * tile : (t + 1) * tile]

    loop(chunks, middle)

    def slot_grad(s):
        rows = agv[landing(s)]
        value = jnp.where(is_live(s), dot(avt[s], rows), 0.0)
        return value.astype(BF16)

    bwd = ring(retb, rin, zb_s, zb_r, -1)
    for i in range(len(order)):
        for k in range(slots):
            retb[i, k] = slot_grad((i + 1) * slots + k)
        bwd[i].start()
    for k in range(slots):
        back[k] = slot_grad(k).astype(F32) + back[prev_b[k]]

    store_o = pltpu.make_async_copy(ov, out_hbm, loc_sem.at[11])
    store_o.start()

    def turn(c):
        agt[:, chunk_rows(c)] = tiles_of(agv, c).astype(F32).T.astype(BF16)

    loop(chunks, turn)

    def hub_part(s):
        value = dot(agt[...], hv[s])
        ps[0, s] = value[:, :half]
        ps[1, s] = value[:, half:]

    loop(sections, hub_part)
    swap_p = remote(ps.at[1 - core], sb, sib_s.at[2], sib_r.at[2], (sib, col))
    swap_p.start()

    def self_grad(c):
        rows = chunk_rows(c)
        pre[rows, :] = lax.dot_general(gv[rows, :], ws[...], NT, preferred_element_type=F32)

    loop(chunks, self_grad)
    swap_p.wait_recv()

    def pair(s):
        rs[s] = (ps[core, s] + sb[s]).astype(BF16)

    loop(sections, pair)

    def hub_c(d):
        return remote(rs.at[:, part_of(chip_of(d)), :], rl.at[chip], c_s.at[d], c_r.at[d], to_chip(d))

    loop(chips, lambda d: hub_c(d).start(), 1)
    for s in range(sections):
        rl[chip, s] = rs[s, own_part, :]
    loop(chips, lambda d: hub_c(d).wait_recv(), 1)
    tot = [rl[0, s].astype(F32) for s in range(sections)]
    for j in range(1, chips):
        tot = [tot[s] + rl[j, s].astype(F32) for s in range(sections)]

    def owners(j):
        for b in range(2):
            value = jnp.zeros((part, half), F32)
            for s in range(sections):
                value = value + jnp.where(hub_ref[s] == j * 2 + b, tot[s], 0.0)
            ow[b, j] = value

    loop(chips, owners)
    swap_o = remote(ow.at[1 - core], osib, sib_s.at[3], sib_r.at[3], (sib, col))
    swap_o.start()
    swap_o.wait_recv()

    def owner_rows(j):
        same = ow[core, j]
        across = osib[j]
        bk[j] = jnp.concatenate(
            [jnp.where(core == 0, same, across), jnp.where(core == 0, across, same)], axis=1
        )

    loop(chips, owner_rows)

    def hub_d(d):
        return remote(bk.at[chip_of(d)], bl.at[own_part, :], d_s.at[d], d_r.at[d], to_chip(d))

    loop(chips, lambda d: hub_d(d).start(), 1)
    bl[own_part, :] = bk[chip]
    loop(chips, lambda d: hub_d(d).wait_recv(), 1)
    pre[pl.ds(0, hub_rows), :] += bl[...].T

    for s in range(slots, total):
        i, k = s // slots - 1, s % slots
        if k == 0:
            bwd[i].wait_recv()
        back[s] = rin[i, k].astype(F32) + back[prev_b[s]]

    store_g = []
    for c in range(chunks):
        for t in range(c * per, (c + 1) * per):
            rows = pl.ds(t * tile, tile)
            fgv[rows, :] = (pre[rows, :] + back[last_b[t]]).astype(BF16)
        rows = pl.ds(c * CHUNK, CHUNK)
        store_g.append(pltpu.make_async_copy(fgv.at[rows, :], fg_hbm.at[rows, :], loc_sem.at[12 + c]))
        store_g[c].start()

    for c in fwd + bwd:
        c.wait_send()
    for c in (swap_b, swap_h, swap_p, swap_o):
        c.wait_send()
    loop(chips, lambda d: hub_a(d).wait_send(), 1)
    loop(chips, lambda d: hub_g(d).wait_send(), 1)
    loop(chips, lambda d: hub_c(d).wait_send(), 1)
    loop(chips, lambda d: hub_d(d).wait_send(), 1)
    store_o.wait()
    for c in store_g:
        c.wait()


def hand_over(a_in, b_in, a_out, b_out, a_buf, b_buf, in_sem, out_sem):
    size = a_in.shape[0] // PIECES
    first, second = [], []
    for n, (src, buf, dst) in enumerate(((a_in, a_buf, a_out), (b_in, b_buf, b_out))):
        for i in range(PIECES):
            rows = pl.ds(i * size, size)
            first.append(pltpu.make_async_copy(src.at[rows, :], buf.at[rows, :], in_sem.at[n, i]))
            second.append(pltpu.make_async_copy(buf.at[rows, :], dst.at[rows, :], out_sem.at[n, i]))
    for c in first:
        c.start()
    for i, c in enumerate(second):
        first[i].wait()
        c.start()
    for c in second:
        c.wait()


def shards(
    features,
    w_self,
    w_neigh,
    bias,
    hub_ids,
    hub_adj,
    send_tile,
    recv_count,
    recv_dst,
    recv_adj,
    cotangent,
):
    n_row, n_col = lax.axis_size("row"), lax.axis_size("col")
    nodes, width = features.shape
    sections, hub_rows = hub_adj.shape[1], hub_adj.shape[3]
    peers, slots, tile = recv_adj.shape[1:4]
    total = peers * slots
    tiles = nodes // tile
    chips = n_row // 2
    part = hub_rows // chips
    half = width // 2
    others = n_col - 1
    vmem, smem, dma = pltpu.VMEM, pltpu.SMEM, pltpu.SemaphoreType.DMA
    spec = lambda space: pl.BlockSpec(memory_space=space)
    results = pl.pallas_call(
        functools.partial(layer_kernel, n_row, n_col),
        out_shape=(
            jax.ShapeDtypeStruct((nodes, width), BF16),
            jax.ShapeDtypeStruct((nodes, width), BF16),
        ),
        in_specs=[spec(pltpu.HBM)] * 11,
        out_specs=(spec(pltpu.HBM), spec(pltpu.HBM)),
        scratch_shapes=[
            smem((slots, peers), jnp.int32),
            smem((peers,), jnp.int32),
            smem((slots, peers), jnp.int32),
            smem((sections,), jnp.int32),
            vmem((width, width), BF16),
            vmem((width, width), BF16),
            vmem((1, width), F32),
            vmem((tiles, tile, width), BF16),
            vmem((sections, nodes, hub_rows), BF16),
            vmem((peers, slots, tile, tile), BF16),
            vmem((total, tile, tile), BF16),
            vmem((nodes, width), BF16),
            vmem((nodes, width), BF16),
            vmem((nodes, width), BF16),
            vmem((tiles, tile, width), BF16),
            vmem((width, nodes), BF16),
            vmem((nodes, width), BF16),
            vmem((nodes, width), F32),
            vmem((nodes, width), F32),
            vmem((nodes, half), F32),
            vmem((others, slots, tile, width), BF16),
            vmem((others, slots, tile, width), BF16),
            vmem((others, slots, tile, width), BF16),
            vmem((others, slots, tile, width), BF16),
            vmem((total + 1, tile, width), F32),
            vmem((total + 1, tile, tile), F32),
            vmem((total + 1, tile, width), F32),
            vmem((chips, part, width), BF16),
            vmem((chips, part, half), BF16),
            vmem((sections, part, half), BF16),
            vmem((sections, hub_rows, width), BF16),
            vmem((2, sections, width, half), F32),
            vmem((sections, width, half), F32),
            vmem((sections, width, half), BF16),
            vmem((chips, sections, part, half), BF16),
            vmem((2, chips, part, half), F32),
            vmem((chips, part, half), F32),
            vmem((chips, part, width), F32),
            vmem((hub_rows, width), F32),
            smem((total,), jnp.int32),
            smem((total,), jnp.int32),
            smem((tiles,), jnp.int32),
            smem((total,), jnp.int32),
            smem((total,), jnp.int32),
            smem((tiles,), jnp.int32),
            dma((12 + nodes // CHUNK,)),
            dma((others,)),
            dma((others,)),
            dma((others,)),
            dma((others,)),
            dma((chips,)),
            dma((chips,)),
            dma((chips,)),
            dma((chips,)),
            dma((chips,)),
            dma((chips,)),
            dma((chips,)),
            dma((chips,)),
            dma((4,)),
            dma((4,)),
        ],
        compiler_params=pltpu.CompilerParams(
            collective_id=0, has_side_effects=True, vmem_limit_bytes=60 * 2**20
        ),
        name="layer",
    )(
        send_tile[0].T,
        recv_count.reshape(peers),
        recv_dst[0].T,
        hub_ids,
        w_self,
        w_neigh,
        bias.reshape(1, width),
        features.reshape(tiles, tile, width),
        hub_adj.reshape(hub_adj.shape[1:]),
        recv_adj.reshape(recv_adj.shape[1:]),
        cotangent,
    )
    return pl.pallas_call(
        hand_over,
        out_shape=[jax.ShapeDtypeStruct((nodes, width), BF16)] * 2,
        in_specs=[spec(pltpu.HBM)] * 2,
        out_specs=[spec(pltpu.HBM)] * 2,
        scratch_shapes=[vmem((nodes, width), BF16)] * 2 + [dma((2, PIECES))] * 2,
        compiler_params=pltpu.CompilerParams(vmem_limit_bytes=60 * 2**20),
        name="hand_over",
    )(*results)


def solution(mesh):
    placed = (
        P(("row", "col"), None),
        P(),
        P(),
        P(),
        P(),
        P(("row", "col"), None, None, None),
        P(("row", "col"), None, None),
        P(("row", "col"), None),
        P(("row", "col"), None, None),
        P(("row", "col"), None, None, None, None),
        P(("row", "col"), None),
    )
    return jax.shard_map(
        shards,
        mesh=mesh,
        in_specs=placed,
        out_specs=(P(("row", "col"), None), P(("row", "col"), None)),
        check_vma=False,
    )
```

```python
import functools

import jax
import jax.numpy as jnp
from jax import lax
from jax.experimental import pallas as pl
from jax.experimental.pallas import tpu as pltpu
from jax.sharding import PartitionSpec as P

MESH = pl.DeviceIdType.MESH
F32 = jnp.float32
BF16 = jnp.bfloat16
CHUNK = 1024
OUT_ROWS = 512
MID = 512
EARLY = 2
PIECES = 4
NT = (((1,), (1,)), ((), ()))


def offsets(n):
    return sorted(range(1, n), key=lambda d: min(d, n - d))


def dot(a, b):
    return jnp.dot(a, b, preferred_element_type=F32)


def layer_kernel(
    n_row,
    n_col,
    send_hbm,
    count_hbm,
    dest_hbm,
    hub_hbm,
    ws_hbm,
    wn_hbm,
    bias_hbm,
    feat_hbm,
    hadj_hbm,
    radj_hbm,
    cot_hbm,
    out_hbm,
    fg_hbm,
    send_ref,
    count_ref,
    dest_ref,
    hub_ref,
    ws,
    wn,
    bias,
    fv,
    hv,
    av,
    avt,
    cv,
    ov,
    gv,
    agv,
    agt,
    fgv,
    pre,
    hs,
    rd,
    outb,
    inc,
    retb,
    rin,
    chain,
    dchain,
    back,
    a_in,
    b_in,
    sel,
    hb,
    ps,
    sb,
    rs,
    rl,
    ow,
    osib,
    bk,
    bl,
    landed,
    prev_f,
    last_f,
    owned,
    prev_b,
    last_b,
    loc_sem,
    zf_s,
    zf_r,
    zb_s,
    zb_r,
    a_s,
    a_r,
    g_s,
    g_r,
    c_s,
    c_r,
    d_s,
    d_r,
    sib_s,
    sib_r,
):
    row = lax.axis_index("row")
    col = lax.axis_index("col")
    chip = row // 2
    core = lax.rem(row, 2)
    sib = chip * 2 + 1 - core
    chips = n_row // 2
    nodes, width = ov.shape
    sections, hub_rows = hv.shape[0], hv.shape[2]
    slots, tile = av.shape[1], av.shape[2]
    tiles = nodes // tile
    part = hub_rows // chips
    half = width // 2
    order = offsets(n_col)
    total = slots * n_col
    chunks = nodes // CHUNK
    per = CHUNK // tile
    mine = pl.ds(pl.multiple_of(core * half, half), half)
    other = pl.ds(pl.multiple_of((1 - core) * half, half), half)
    own_part = pl.ds(pl.multiple_of(chip * part, part), part)

    def tile_rows(t):
        return pl.ds(pl.multiple_of(t * tile, tile), tile)

    def chunk_rows(c):
        return pl.ds(pl.multiple_of(c * CHUNK, CHUNK), CHUNK)

    def get(ref, first, number):
        return jnp.concatenate([ref[first + t] for t in range(number)], axis=0)

    def put(ref, first, value):
        for t in range(value.shape[0] // tile):
            ref[first + t] = value[t * tile : (t + 1) * tile]

    def loop(n, body, start=0):
        def run(i, carry):
            body(i)
            return carry

        lax.fori_loop(start, n, run, 0)

    def remote(src, dst, send, recv, to):
        return pltpu.make_async_remote_copy(
            src_ref=src, dst_ref=dst, send_sem=send, recv_sem=recv, device_id=to, device_id_type=MESH
        )

    def to_col(d):
        return (row, lax.rem(col + d, n_col))

    def chip_of(d):
        return lax.rem(chip + d, chips)

    def to_chip(d):
        return (chip_of(d) * 2 + core, col)

    def part_of(j):
        return pl.ds(pl.multiple_of(j * part, part), part)

    barrier = pltpu.get_barrier_semaphore()
    for d in order:
        pl.semaphore_signal(barrier, inc=1, device_id=to_col(d), device_id_type=MESH)

    def greet(d):
        pl.semaphore_signal(barrier, inc=1, device_id=to_chip(d), device_id_type=MESH)

    loop(chips, greet, 1)
    pl.semaphore_signal(barrier, inc=1, device_id=(sib, col), device_id_type=MESH)

    pairs = (
        (send_hbm, send_ref),
        (feat_hbm, fv),
        (dest_hbm, dest_ref),
        (count_hbm, count_ref),
        (hub_hbm, hub_ref),
        (ws_hbm, ws),
        (bias_hbm, bias),
        (radj_hbm, av),
        (hadj_hbm, hv),
        (wn_hbm, wn),
        (cot_hbm, cv),
    )
    loads = [pltpu.make_async_copy(src, dst, loc_sem.at[i]) for i, (src, dst) in enumerate(pairs)]
    for c in loads:
        c.start()
    loads[0].wait()
    loads[1].wait()

    def stage(i, d):
        to = lax.rem(col + d, n_col)
        for k in range(slots):
            outb[i, k] = fv[send_ref[k, to]]

    stage(0, order[0])
    pl.semaphore_wait(barrier, n_col - 1 + chips - 1 + 1)

    def ring(buf, land, send, recv, sign):
        return [
            remote(buf.at[i], land.at[i], send.at[i], recv.at[i], to_col(d if sign > 0 else n_col - d))
            for i, d in enumerate(order)
        ]

    fwd = ring(outb, inc, zf_s, zf_r, 1)
    fwd[0].start()

    per_tile = tile // part

    def hub_of(j):
        return fv.at[j // per_tile, part_of(lax.rem(j, per_tile)), :]

    def hub_a(d):
        return remote(hub_of(chip_of(d)), a_in.at[chip], a_s.at[d], a_r.at[d], to_chip(d))

    loop(chips, lambda d: hub_a(d).start(), 1)
    a_in[chip] = fv[chip // per_tile, part_of(lax.rem(chip, per_tile)), :]
    for i in range(1, len(order)):
        stage(i, order[i])
        fwd[i].start()

    loads[5].wait()
    loads[6].wait()

    def self_part(c):
        put(pre, c * per, dot(get(fv, c * per, per), ws[...]) + bias[...])

    loop(chunks, self_part)

    loop(chips, lambda d: hub_a(d).wait_recv(), 1)
    swap_b = remote(a_in.at[:, :, other], b_in, sib_s.at[0], sib_r.at[0], (sib, col))
    swap_b.start()

    for c in loads[2:5]:
        c.wait()

    def offset(s):
        return ([0] + order)[s // slots]

    def weights(s):
        return lax.rem(col + n_col - offset(s), n_col), s % slots

    def landing(s):
        p, k = weights(s)
        return dest_ref[k, p]

    def offered(s):
        return send_ref[s % slots, lax.rem(col + offset(s), n_col)]

    def is_live(s):
        p, k = weights(s)
        return k < count_ref[p]

    for s in range(total):
        landed[s] = jnp.where(is_live(s), landing(s), -1)
        owned[s] = offered(s)

    def link(keys, prev, last):
        def before(s):
            key = keys[s]
            found = total
            for t in range(total):
                found = jnp.where((t < s) & (keys[t] == key), t, found)
            prev[s] = found

        def final(n):
            found = total
            for t in range(total):
                found = jnp.where(keys[t] == n, t, found)
            last[n] = found

        loop(total, before)
        loop(tiles, final)

    link(landed, prev_f, last_f)
    link(owned, prev_b, last_b)
    chain[total] = jnp.zeros((tile, width), F32)
    back[total] = jnp.zeros((tile, width), F32)
    dchain[total] = jnp.zeros((tile, tile), F32)

    swap_b.wait_recv()
    for s in range(sections):
        h = hub_ref[s]
        h_chip = h // 2
        h_core = h - 2 * h_chip
        both = a_in[h_chip].astype(F32)
        same = jnp.where(core == 0, both[:, :half], both[:, half:])
        across = b_in[h_chip].astype(F32)
        sel[s] = jnp.where(h_core == core, same, across).astype(BF16)
    spread = hb.at[:, own_part, mine]

    def hub_g(d):
        return remote(sel, spread, g_s.at[d], g_r.at[d], to_chip(d))

    loop(chips, lambda d: hub_g(d).start(), 1)
    for s in range(sections):
        hb[s, own_part, mine] = sel[s]

    loads[7].wait()
    ones_t = jnp.ones((tile, tile), BF16)

    for s in range(total):
        p, k = weights(s)
        w = av[p, k]
        dchain[s] = dot(w, ones_t) + dchain[prev_f[s]]
        avt[s] = w.astype(F32).T.astype(BF16)

    loads[8].wait()
    ones_h = jnp.ones((hub_rows, half), BF16)

    def degrees(c):
        rows = chunk_rows(c)
        deg = 1.0 + jnp.concatenate([dchain[last_f[c * per + t]] for t in range(per)], axis=0)
        for s in range(sections):
            deg = deg + dot(hv[s, rows, :], ones_h)
        put(rd, c * per, 1.0 / deg)

    loop(chunks, degrees)

    loop(chips, lambda d: hub_g(d).wait_recv(), 1)
    swap_h = remote(hb.at[:, :, mine], hb.at[:, :, mine], sib_s.at[1], sib_r.at[1], (sib, col))
    swap_h.start()
    swap_h.wait_recv()

    def hub_sum(c):
        rows = chunk_rows(c)
        acc = dot(hv[0, rows, :], hb[0])
        for s in range(1, sections):
            acc = acc + dot(hv[s, rows, :], hb[s])
        put(hs, c * per, acc)

    loop(chunks, hub_sum)

    for s in range(total):
        i, k = s // slots - 1, s % slots
        p, _ = weights(s)
        if i < 0:
            arrived = fv[offered(s)]
        else:
            if k == 0:
                fwd[i].wait_recv()
            arrived = inc[i, k]
        chain[s] = dot(av[p, k], arrived) + chain[prev_f[s]]
    loads[9].wait()
    loads[10].wait()

    def node(raw, inv, own, cot):
        inv = jnp.concatenate([inv] * (width // half), axis=1)
        agg = (raw * inv).astype(BF16)
        x = own + dot(agg, wn[...])
        sig = 0.5 * jnp.tanh(0.5 * x) + 0.5
        grad = (cot.astype(F32) * sig * (1.0 + x * (1.0 - sig))).astype(BF16)
        back_grad = lax.dot_general(grad, wn[...], NT, preferred_element_type=F32)
        return x * sig, grad, (back_grad * inv).astype(BF16)

    def at_tiles(ns):
        def pick(ref):
            return jnp.concatenate([ref[n] for n in ns], axis=0)

        raw = pick(hs) + jnp.concatenate([chain[last_f[n]] for n in ns], axis=0)
        return node(raw, pick(rd), pick(pre), pick(cv))

    def middle(c):
        first = c * (MID // tile)
        rows = pl.ds(c * MID, MID)
        value, grad, scaled = at_tiles([first + t for t in range(MID // tile)])
        ov[rows, :] = value.astype(BF16)
        gv[rows, :] = grad
        put(agv, first, scaled)

    def slot_grad(s, rows):
        return jnp.where(is_live(s), dot(avt[s], rows), 0.0).astype(BF16)

    bwd = ring(retb, rin, zb_s, zb_r, -1)
    for i in range(EARLY):
        ready = [(i + 1) * slots + k for k in range(slots)]
        _, _, rows = at_tiles([landing(s) for s in ready])
        for k, s in enumerate(ready):
            retb[i, k] = slot_grad(s, rows[k * tile : (k + 1) * tile])
        bwd[i].start()

    for c in range(nodes // MID):
        middle(c)

    for i in range(EARLY, len(order)):
        for k in range(slots):
            s = (i + 1) * slots + k
            retb[i, k] = slot_grad(s, agv[landing(s)])
        bwd[i].start()
    for k in range(slots):
        back[k] = slot_grad(k, agv[landing(k)]).astype(F32) + back[prev_b[k]]

    store_o = pltpu.make_async_copy(ov, out_hbm, loc_sem.at[11])
    store_o.start()

    def turn(c):
        agt[:, chunk_rows(c)] = get(agv, c * per, per).astype(F32).T.astype(BF16)

    loop(chunks, turn)

    def hub_part(s):
        value = dot(agt[...], hv[s])
        ps[0, s] = value[:, :half]
        ps[1, s] = value[:, half:]

    loop(sections, hub_part)
    swap_p = remote(ps.at[1 - core], sb, sib_s.at[2], sib_r.at[2], (sib, col))
    swap_p.start()

    def self_grad(c):
        rows = chunk_rows(c)
        put(pre, c * per, lax.dot_general(gv[rows, :], ws[...], NT, preferred_element_type=F32))

    loop(chunks, self_grad)
    swap_p.wait_recv()

    def pair(s):
        rs[s] = (ps[core, s] + sb[s]).astype(BF16)

    loop(sections, pair)

    def hub_c(d):
        return remote(rs.at[:, part_of(chip_of(d)), :], rl.at[chip], c_s.at[d], c_r.at[d], to_chip(d))

    loop(chips, lambda d: hub_c(d).start(), 1)
    for s in range(sections):
        rl[chip, s] = rs[s, own_part, :]
    loop(chips, lambda d: hub_c(d).wait_recv(), 1)
    tot = [rl[0, s].astype(F32) for s in range(sections)]
    for j in range(1, chips):
        tot = [tot[s] + rl[j, s].astype(F32) for s in range(sections)]

    def owners(j):
        for b in range(2):
            value = jnp.zeros((part, half), F32)
            for s in range(sections):
                value = value + jnp.where(hub_ref[s] == j * 2 + b, tot[s], 0.0)
            ow[b, j] = value

    loop(chips, owners)
    swap_o = remote(ow.at[1 - core], osib, sib_s.at[3], sib_r.at[3], (sib, col))
    swap_o.start()
    swap_o.wait_recv()

    def owner_rows(j):
        same = ow[core, j]
        across = osib[j]
        bk[j] = jnp.concatenate(
            [jnp.where(core == 0, same, across), jnp.where(core == 0, across, same)], axis=1
        )

    loop(chips, owner_rows)

    def hub_d(d):
        return remote(bk.at[chip_of(d)], bl.at[own_part, :], d_s.at[d], d_r.at[d], to_chip(d))

    loop(chips, lambda d: hub_d(d).start(), 1)
    bl[own_part, :] = bk[chip]
    loop(chips, lambda d: hub_d(d).wait_recv(), 1)
    put(pre, 0, get(pre, 0, hub_rows // tile) + bl[...].T)

    for c in fwd:
        c.wait_send()
    for c in (swap_b, swap_h, swap_p, swap_o):
        c.wait_send()
    for sent in (hub_a, hub_g, hub_c, hub_d):
        loop(chips, lambda d, sent=sent: sent(d).wait_send(), 1)
    store_o.wait()

    for s in range(slots, total):
        i, k = s // slots - 1, s % slots
        if k == 0:
            bwd[i].wait_recv()
        back[s] = rin[i, k].astype(F32) + back[prev_b[s]]

    store_g = []
    for c in range(nodes // OUT_ROWS):
        for t in range(c * OUT_ROWS // tile, (c + 1) * OUT_ROWS // tile):
            rows = pl.ds(t * tile, tile)
            fgv[rows, :] = (pre[t] + back[last_b[t]]).astype(BF16)
        rows = pl.ds(c * OUT_ROWS, OUT_ROWS)
        store_g.append(pltpu.make_async_copy(fgv.at[rows, :], fg_hbm.at[rows, :], loc_sem.at[12 + c]))
        store_g[c].start()
    for c in bwd:
        c.wait_send()
    for c in store_g:
        c.wait()


def hand_over(a_in, b_in, a_out, b_out, a_buf, b_buf, in_sem, out_sem):
    size = a_in.shape[0] // PIECES
    first, second = [], []
    for n, (src, buf, dst) in enumerate(((a_in, a_buf, a_out), (b_in, b_buf, b_out))):
        for i in range(PIECES):
            rows = pl.ds(i * size, size)
            first.append(pltpu.make_async_copy(src.at[rows, :], buf.at[rows, :], in_sem.at[n, i]))
            second.append(pltpu.make_async_copy(buf.at[rows, :], dst.at[rows, :], out_sem.at[n, i]))
    for c in first:
        c.start()
    for i, c in enumerate(second):
        first[i].wait()
        c.start()
    for c in second:
        c.wait()


def shards(
    features,
    w_self,
    w_neigh,
    bias,
    hub_ids,
    hub_adj,
    send_tile,
    recv_count,
    recv_dst,
    recv_adj,
    cotangent,
):
    n_row, n_col = lax.axis_size("row"), lax.axis_size("col")
    nodes, width = features.shape
    sections, hub_rows = hub_adj.shape[1], hub_adj.shape[3]
    peers, slots, tile = recv_adj.shape[1:4]
    total = peers * slots
    tiles = nodes // tile
    chips = n_row // 2
    part = hub_rows // chips
    half = width // 2
    others = n_col - 1
    vmem, smem, dma = pltpu.VMEM, pltpu.SMEM, pltpu.SemaphoreType.DMA
    spec = lambda space: pl.BlockSpec(memory_space=space)
    results = pl.pallas_call(
        functools.partial(layer_kernel, n_row, n_col),
        out_shape=(
            jax.ShapeDtypeStruct((nodes, width), BF16),
            jax.ShapeDtypeStruct((nodes, width), BF16),
        ),
        in_specs=[spec(pltpu.HBM)] * 11,
        out_specs=(spec(pltpu.HBM), spec(pltpu.HBM)),
        scratch_shapes=[
            smem((slots, peers), jnp.int32),
            smem((peers,), jnp.int32),
            smem((slots, peers), jnp.int32),
            smem((sections,), jnp.int32),
            vmem((width, width), BF16),
            vmem((width, width), BF16),
            vmem((1, width), F32),
            vmem((tiles, tile, width), BF16),
            vmem((sections, nodes, hub_rows), BF16),
            vmem((peers, slots, tile, tile), BF16),
            vmem((total, tile, tile), BF16),
            vmem((tiles, tile, width), BF16),
            vmem((nodes, width), BF16),
            vmem((nodes, width), BF16),
            vmem((tiles, tile, width), BF16),
            vmem((width, nodes), BF16),
            vmem((nodes, width), BF16),
            vmem((tiles, tile, width), F32),
            vmem((tiles, tile, width), F32),
            vmem((tiles, tile, half), F32),
            vmem((others, slots, tile, width), BF16),
            vmem((others, slots, tile, width), BF16),
            vmem((others, slots, tile, width), BF16),
            vmem((others, slots, tile, width), BF16),
            vmem((total + 1, tile, width), F32),
            vmem((total + 1, tile, tile), F32),
            vmem((total + 1, tile, width), F32),
            vmem((chips, part, width), BF16),
            vmem((chips, part, half), BF16),
            vmem((sections, part, half), BF16),
            vmem((sections, hub_rows, width), BF16),
            vmem((2, sections, width, half), F32),
            vmem((sections, width, half), F32),
            vmem((sections, width, half), BF16),
            vmem((chips, sections, part, half), BF16),
            vmem((2, chips, part, half), F32),
            vmem((chips, part, half), F32),
            vmem((chips, part, width), F32),
            vmem((hub_rows, width), F32),
            smem((total,), jnp.int32),
            smem((total,), jnp.int32),
            smem((tiles,), jnp.int32),
            smem((total,), jnp.int32),
            smem((total,), jnp.int32),
            smem((tiles,), jnp.int32),
            dma((12 + nodes // OUT_ROWS,)),
            dma((others,)),
            dma((others,)),
            dma((others,)),
            dma((others,)),
            dma((chips,)),
            dma((chips,)),
            dma((chips,)),
            dma((chips,)),
            dma((chips,)),
            dma((chips,)),
            dma((chips,)),
            dma((chips,)),
            dma((4,)),
            dma((4,)),
        ],
        compiler_params=pltpu.CompilerParams(
            collective_id=0, has_side_effects=True, vmem_limit_bytes=60 * 2**20
        ),
        name="layer",
    )(
        send_tile[0].T,
        recv_count.reshape(peers),
        recv_dst[0].T,
        hub_ids,
        w_self,
        w_neigh,
        bias.reshape(1, width),
        features.reshape(tiles, tile, width),
        hub_adj.reshape(hub_adj.shape[1:]),
        recv_adj.reshape(recv_adj.shape[1:]),
        cotangent.reshape(tiles, tile, width),
    )
    return pl.pallas_call(
        hand_over,
        out_shape=[jax.ShapeDtypeStruct((nodes, width), BF16)] * 2,
        in_specs=[spec(pltpu.HBM)] * 2,
        out_specs=[spec(pltpu.HBM)] * 2,
        scratch_shapes=[vmem((nodes, width), BF16)] * 2 + [dma((2, PIECES))] * 2,
        compiler_params=pltpu.CompilerParams(vmem_limit_bytes=60 * 2**20),
        name="hand_over",
    )(*results)


def solution(mesh):
    placed = (
        P(("row", "col"), None),
        P(),
        P(),
        P(),
        P(),
        P(("row", "col"), None, None, None),
        P(("row", "col"), None, None),
        P(("row", "col"), None),
        P(("row", "col"), None, None),
        P(("row", "col"), None, None, None, None),
        P(("row", "col"), None),
    )
    return jax.shard_map(
        shards,
        mesh=mesh,
        in_specs=placed,
        out_specs=(P(("row", "col"), None), P(("row", "col"), None)),
        check_vma=False,
    )
```

```python
import functools

import jax
import jax.numpy as jnp
from jax import lax
from jax.experimental import pallas as pl
from jax.experimental.pallas import tpu as pltpu
from jax.sharding import PartitionSpec as P

MESH = pl.DeviceIdType.MESH
F32 = jnp.float32
BF16 = jnp.bfloat16
CHUNK = 1024
OUT_ROWS = 512
MID = 512
EARLY = 2
PIECES = 4
NT = (((1,), (1,)), ((), ()))


def offsets(n):
    return sorted(range(1, n), key=lambda d: min(d, n - d))


def dot(a, b):
    return jnp.dot(a, b, preferred_element_type=F32)


def layer_kernel(
    n_row,
    n_col,
    send_hbm,
    count_hbm,
    dest_hbm,
    hub_hbm,
    ws_hbm,
    wn_hbm,
    bias_hbm,
    feat_hbm,
    hadj_hbm,
    radj_hbm,
    cot_hbm,
    out_hbm,
    fg_hbm,
    send_ref,
    count_ref,
    dest_ref,
    hub_ref,
    ws,
    wn,
    bias,
    fv,
    hv,
    av,
    avt,
    cv,
    ov,
    gv,
    agv,
    agt,
    fgv,
    pre,
    hs,
    rd,
    outb,
    inc,
    retb,
    rin,
    chain,
    dchain,
    back,
    a_in,
    b_in,
    sel,
    hb,
    ps,
    sb,
    rs,
    rl,
    ow,
    osib,
    bk,
    bl,
    landed,
    prev_f,
    last_f,
    owned,
    prev_b,
    last_b,
    loc_sem,
    zf_s,
    zf_r,
    zb_s,
    zb_r,
    a_s,
    a_r,
    g_s,
    g_r,
    c_s,
    c_r,
    d_s,
    d_r,
    sib_s,
    sib_r,
):
    row = lax.axis_index("row")
    col = lax.axis_index("col")
    chip = row // 2
    core = lax.rem(row, 2)
    sib = chip * 2 + 1 - core
    chips = n_row // 2
    nodes, width = ov.shape
    sections, hub_rows = hv.shape[0], hv.shape[2]
    slots, tile = av.shape[1], av.shape[2]
    tiles = nodes // tile
    part = hub_rows // chips
    half = width // 2
    order = offsets(n_col)
    total = slots * n_col
    chunks = nodes // CHUNK
    per = CHUNK // tile
    mine = pl.ds(pl.multiple_of(core * half, half), half)
    other = pl.ds(pl.multiple_of((1 - core) * half, half), half)
    own_part = pl.ds(pl.multiple_of(chip * part, part), part)

    def tile_rows(t):
        return pl.ds(pl.multiple_of(t * tile, tile), tile)

    def chunk_rows(c):
        return pl.ds(pl.multiple_of(c * CHUNK, CHUNK), CHUNK)

    def get(ref, first, number):
        return jnp.concatenate([ref[first + t] for t in range(number)], axis=0)

    def put(ref, first, value):
        for t in range(value.shape[0] // tile):
            ref[first + t] = value[t * tile : (t + 1) * tile]

    def loop(n, body, start=0):
        def run(i, carry):
            body(i)
            return carry

        lax.fori_loop(start, n, run, 0)

    def remote(src, dst, send, recv, to):
        return pltpu.make_async_remote_copy(
            src_ref=src, dst_ref=dst, send_sem=send, recv_sem=recv, device_id=to, device_id_type=MESH
        )

    def to_col(d):
        return (row, lax.rem(col + d, n_col))

    def chip_of(d):
        return lax.rem(chip + d, chips)

    def to_chip(d):
        return (chip_of(d) * 2 + core, col)

    def part_of(j):
        return pl.ds(pl.multiple_of(j * part, part), part)

    barrier = pltpu.get_barrier_semaphore()
    for d in order:
        pl.semaphore_signal(barrier, inc=1, device_id=to_col(d), device_id_type=MESH)

    def greet(d):
        pl.semaphore_signal(barrier, inc=1, device_id=to_chip(d), device_id_type=MESH)

    loop(chips, greet, 1)
    pl.semaphore_signal(barrier, inc=1, device_id=(sib, col), device_id_type=MESH)

    pairs = (
        (send_hbm, send_ref),
        (feat_hbm, fv),
        (dest_hbm, dest_ref),
        (count_hbm, count_ref),
        (hub_hbm, hub_ref),
        (ws_hbm, ws),
        (bias_hbm, bias),
        (radj_hbm, av),
        (hadj_hbm, hv),
        (wn_hbm, wn),
        (cot_hbm, cv),
    )
    loads = [pltpu.make_async_copy(src, dst, loc_sem.at[i]) for i, (src, dst) in enumerate(pairs)]
    for c in loads:
        c.start()
    loads[0].wait()
    loads[1].wait()

    def stage(i, d):
        to = lax.rem(col + d, n_col)
        for k in range(slots):
            outb[i, k] = fv[send_ref[k, to]]

    stage(0, order[0])
    stage(1, order[1])
    pl.semaphore_wait(barrier, n_col - 1 + chips - 1 + 1)

    def ring(buf, land, send, recv, sign):
        return [
            remote(buf.at[i], land.at[i], send.at[i], recv.at[i], to_col(d if sign > 0 else n_col - d))
            for i, d in enumerate(order)
        ]

    fwd = ring(outb, inc, zf_s, zf_r, 1)
    fwd[0].start()
    fwd[1].start()

    per_tile = tile // part

    def hub_of(j):
        return fv.at[j // per_tile, part_of(lax.rem(j, per_tile)), :]

    def hub_a(d):
        return remote(hub_of(chip_of(d)), a_in.at[chip], a_s.at[d], a_r.at[d], to_chip(d))

    loop(chips, lambda d: hub_a(d).start(), 1)
    a_in[chip] = fv[chip // per_tile, part_of(lax.rem(chip, per_tile)), :]
    for i in range(2, len(order)):
        stage(i, order[i])
        fwd[i].start()

    loads[5].wait()
    loads[6].wait()

    def self_part(c):
        put(pre, c * per, dot(get(fv, c * per, per), ws[...]) + bias[...])

    loop(chunks, self_part)

    loop(chips, lambda d: hub_a(d).wait_recv(), 1)
    swap_b = remote(a_in.at[:, :, other], b_in, sib_s.at[0], sib_r.at[0], (sib, col))
    swap_b.start()

    for c in loads[2:5]:
        c.wait()

    def offset(s):
        return ([0] + order)[s // slots]

    def weights(s):
        return lax.rem(col + n_col - offset(s), n_col), s % slots

    def landing(s):
        p, k = weights(s)
        return dest_ref[k, p]

    def offered(s):
        return send_ref[s % slots, lax.rem(col + offset(s), n_col)]

    def is_live(s):
        p, k = weights(s)
        return k < count_ref[p]

    for s in range(total):
        landed[s] = jnp.where(is_live(s), landing(s), -1)
        owned[s] = offered(s)

    def link(keys, prev, last):
        def before(s):
            key = keys[s]
            found = total
            for t in range(total):
                found = jnp.where((t < s) & (keys[t] == key), t, found)
            prev[s] = found

        def final(n):
            found = total
            for t in range(total):
                found = jnp.where(keys[t] == n, t, found)
            last[n] = found

        loop(total, before)
        loop(tiles, final)

    link(landed, prev_f, last_f)
    link(owned, prev_b, last_b)
    chain[total] = jnp.zeros((tile, width), F32)
    back[total] = jnp.zeros((tile, width), F32)
    dchain[total] = jnp.zeros((tile, tile), F32)

    swap_b.wait_recv()
    for s in range(sections):
        h = hub_ref[s]
        h_chip = h // 2
        h_core = h - 2 * h_chip
        both = a_in[h_chip].astype(F32)
        same = jnp.where(core == 0, both[:, :half], both[:, half:])
        across = b_in[h_chip].astype(F32)
        sel[s] = jnp.where(h_core == core, same, across).astype(BF16)
    spread = hb.at[:, own_part, mine]

    def hub_g(d):
        return remote(sel, spread, g_s.at[d], g_r.at[d], to_chip(d))

    loop(chips, lambda d: hub_g(d).start(), 1)
    for s in range(sections):
        hb[s, own_part, mine] = sel[s]

    loads[7].wait()
    ones_t = jnp.ones((tile, tile), BF16)

    for s in range(total):
        p, k = weights(s)
        w = av[p, k]
        dchain[s] = dot(w, ones_t) + dchain[prev_f[s]]
        avt[s] = w.astype(F32).T.astype(BF16)

    loads[8].wait()
    ones_h = jnp.ones((hub_rows, half), BF16)

    def degrees(c):
        rows = chunk_rows(c)
        deg = 1.0 + jnp.concatenate([dchain[last_f[c * per + t]] for t in range(per)], axis=0)
        for s in range(sections):
            deg = deg + dot(hv[s, rows, :], ones_h)
        put(rd, c * per, 1.0 / deg)

    loop(chunks, degrees)

    loop(chips, lambda d: hub_g(d).wait_recv(), 1)
    swap_h = remote(hb.at[:, :, mine], hb.at[:, :, mine], sib_s.at[1], sib_r.at[1], (sib, col))
    swap_h.start()
    swap_h.wait_recv()

    def hub_sum(c):
        rows = chunk_rows(c)
        acc = dot(hv[0, rows, :], hb[0])
        for s in range(1, sections):
            acc = acc + dot(hv[s, rows, :], hb[s])
        put(hs, c * per, acc)

    loop(chunks, hub_sum)

    for s in range(total):
        i, k = s // slots - 1, s % slots
        p, _ = weights(s)
        if i < 0:
            arrived = fv[offered(s)]
        else:
            if k == 0:
                fwd[i].wait_recv()
            arrived = inc[i, k]
        chain[s] = dot(av[p, k], arrived) + chain[prev_f[s]]
    loads[9].wait()
    loads[10].wait()

    def node(raw, inv, own, cot):
        inv = jnp.concatenate([inv] * (width // half), axis=1)
        agg = (raw * inv).astype(BF16)
        x = own + dot(agg, wn[...])
        sig = 0.5 * jnp.tanh(0.5 * x) + 0.5
        grad = (cot.astype(F32) * sig * (1.0 + x * (1.0 - sig))).astype(BF16)
        back_grad = lax.dot_general(grad, wn[...], NT, preferred_element_type=F32)
        return x * sig, grad, (back_grad * inv).astype(BF16)

    def at_tiles(ns):
        def pick(ref):
            return jnp.concatenate([ref[n] for n in ns], axis=0)

        raw = pick(hs) + jnp.concatenate([chain[last_f[n]] for n in ns], axis=0)
        return node(raw, pick(rd), pick(pre), pick(cv))

    def middle(c):
        first = c * (MID // tile)
        rows = pl.ds(c * MID, MID)
        value, grad, scaled = at_tiles([first + t for t in range(MID // tile)])
        ov[rows, :] = value.astype(BF16)
        gv[rows, :] = grad
        put(agv, first, scaled)

    def slot_grad(s, rows):
        return jnp.where(is_live(s), dot(avt[s], rows), 0.0).astype(BF16)

    bwd = ring(retb, rin, zb_s, zb_r, -1)
    for i in range(EARLY):
        ready = [(i + 1) * slots + k for k in range(slots)]
        _, _, rows = at_tiles([landing(s) for s in ready])
        for k, s in enumerate(ready):
            retb[i, k] = slot_grad(s, rows[k * tile : (k + 1) * tile])
        bwd[i].start()

    for c in range(nodes // MID):
        middle(c)

    for i in range(EARLY, len(order)):
        for k in range(slots):
            s = (i + 1) * slots + k
            retb[i, k] = slot_grad(s, agv[landing(s)])
        bwd[i].start()
    for k in range(slots):
        back[k] = slot_grad(k, agv[landing(k)]).astype(F32) + back[prev_b[k]]

    store_o = pltpu.make_async_copy(ov, out_hbm, loc_sem.at[11])
    store_o.start()

    def turn(c):
        agt[:, chunk_rows(c)] = get(agv, c * per, per).astype(F32).T.astype(BF16)

    loop(chunks, turn)

    def hub_part(s):
        value = dot(agt[...], hv[s])
        ps[0, s] = value[:, :half]
        ps[1, s] = value[:, half:]

    loop(sections, hub_part)
    swap_p = remote(ps.at[1 - core], sb, sib_s.at[2], sib_r.at[2], (sib, col))
    swap_p.start()

    def self_grad(c):
        rows = chunk_rows(c)
        put(pre, c * per, lax.dot_general(gv[rows, :], ws[...], NT, preferred_element_type=F32))

    loop(chunks, self_grad)
    swap_p.wait_recv()

    def pair(s):
        rs[s] = (ps[core, s] + sb[s]).astype(BF16)

    loop(sections, pair)

    def hub_c(d):
        return remote(rs.at[:, part_of(chip_of(d)), :], rl.at[chip], c_s.at[d], c_r.at[d], to_chip(d))

    loop(chips, lambda d: hub_c(d).start(), 1)
    for s in range(sections):
        rl[chip, s] = rs[s, own_part, :]
    loop(chips, lambda d: hub_c(d).wait_recv(), 1)
    tot = [rl[0, s].astype(F32) for s in range(sections)]
    for j in range(1, chips):
        tot = [tot[s] + rl[j, s].astype(F32) for s in range(sections)]

    def owners(j):
        for b in range(2):
            value = jnp.zeros((part, half), F32)
            for s in range(sections):
                value = value + jnp.where(hub_ref[s] == j * 2 + b, tot[s], 0.0)
            ow[b, j] = value

    loop(chips, owners)
    swap_o = remote(ow.at[1 - core], osib, sib_s.at[3], sib_r.at[3], (sib, col))
    swap_o.start()
    swap_o.wait_recv()

    def owner_rows(j):
        same = ow[core, j]
        across = osib[j]
        bk[j] = jnp.concatenate(
            [jnp.where(core == 0, same, across), jnp.where(core == 0, across, same)], axis=1
        )

    loop(chips, owner_rows)

    def hub_d(d):
        return remote(bk.at[chip_of(d)], bl.at[own_part, :], d_s.at[d], d_r.at[d], to_chip(d))

    loop(chips, lambda d: hub_d(d).start(), 1)
    bl[own_part, :] = bk[chip]
    loop(chips, lambda d: hub_d(d).wait_recv(), 1)
    put(pre, 0, get(pre, 0, hub_rows // tile) + bl[...].T)

    for c in fwd:
        c.wait_send()
    for c in (swap_b, swap_h, swap_p, swap_o):
        c.wait_send()
    for sent in (hub_a, hub_g, hub_c, hub_d):
        loop(chips, lambda d, sent=sent: sent(d).wait_send(), 1)
    store_o.wait()

    for s in range(slots, total):
        i, k = s // slots - 1, s % slots
        if k == 0:
            bwd[i].wait_recv()
        back[s] = rin[i, k].astype(F32) + back[prev_b[s]]

    store_g = []
    for c in range(nodes // OUT_ROWS):
        for t in range(c * OUT_ROWS // tile, (c + 1) * OUT_ROWS // tile):
            rows = pl.ds(t * tile, tile)
            fgv[rows, :] = (pre[t] + back[last_b[t]]).astype(BF16)
        rows = pl.ds(c * OUT_ROWS, OUT_ROWS)
        store_g.append(pltpu.make_async_copy(fgv.at[rows, :], fg_hbm.at[rows, :], loc_sem.at[12 + c]))
        store_g[c].start()
    for c in bwd:
        c.wait_send()
    for c in store_g:
        c.wait()


def hand_over(a_in, b_in, a_out, b_out, a_buf, b_buf, in_sem, out_sem):
    size = a_in.shape[0] // PIECES
    first, second = [], []
    for n, (src, buf, dst) in enumerate(((a_in, a_buf, a_out), (b_in, b_buf, b_out))):
        for i in range(PIECES):
            rows = pl.ds(i * size, size)
            first.append(pltpu.make_async_copy(src.at[rows, :], buf.at[rows, :], in_sem.at[n, i]))
            second.append(pltpu.make_async_copy(buf.at[rows, :], dst.at[rows, :], out_sem.at[n, i]))
    for c in first:
        c.start()
    for i, c in enumerate(second):
        first[i].wait()
        c.start()
    for c in second:
        c.wait()


def shards(
    features,
    w_self,
    w_neigh,
    bias,
    hub_ids,
    hub_adj,
    send_tile,
    recv_count,
    recv_dst,
    recv_adj,
    cotangent,
):
    n_row, n_col = lax.axis_size("row"), lax.axis_size("col")
    nodes, width = features.shape
    sections, hub_rows = hub_adj.shape[1], hub_adj.shape[3]
    peers, slots, tile = recv_adj.shape[1:4]
    total = peers * slots
    tiles = nodes // tile
    chips = n_row // 2
    part = hub_rows // chips
    half = width // 2
    others = n_col - 1
    vmem, smem, dma = pltpu.VMEM, pltpu.SMEM, pltpu.SemaphoreType.DMA
    spec = lambda space: pl.BlockSpec(memory_space=space)
    results = pl.pallas_call(
        functools.partial(layer_kernel, n_row, n_col),
        out_shape=(
            jax.ShapeDtypeStruct((nodes, width), BF16),
            jax.ShapeDtypeStruct((nodes, width), BF16),
        ),
        in_specs=[spec(pltpu.HBM)] * 11,
        out_specs=(spec(pltpu.HBM), spec(pltpu.HBM)),
        scratch_shapes=[
            smem((slots, peers), jnp.int32),
            smem((peers,), jnp.int32),
            smem((slots, peers), jnp.int32),
            smem((sections,), jnp.int32),
            vmem((width, width), BF16),
            vmem((width, width), BF16),
            vmem((1, width), F32),
            vmem((tiles, tile, width), BF16),
            vmem((sections, nodes, hub_rows), BF16),
            vmem((peers, slots, tile, tile), BF16),
            vmem((total, tile, tile), BF16),
            vmem((tiles, tile, width), BF16),
            vmem((nodes, width), BF16),
            vmem((nodes, width), BF16),
            vmem((tiles, tile, width), BF16),
            vmem((width, nodes), BF16),
            vmem((nodes, width), BF16),
            vmem((tiles, tile, width), F32),
            vmem((tiles, tile, width), F32),
            vmem((tiles, tile, half), F32),
            vmem((others, slots, tile, width), BF16),
            vmem((others, slots, tile, width), BF16),
            vmem((others, slots, tile, width), BF16),
            vmem((others, slots, tile, width), BF16),
            vmem((total + 1, tile, width), F32),
            vmem((total + 1, tile, tile), F32),
            vmem((total + 1, tile, width), F32),
            vmem((chips, part, width), BF16),
            vmem((chips, part, half), BF16),
            vmem((sections, part, half), BF16),
            vmem((sections, hub_rows, width), BF16),
            vmem((2, sections, width, half), F32),
            vmem((sections, width, half), F32),
            vmem((sections, width, half), BF16),
            vmem((chips, sections, part, half), BF16),
            vmem((2, chips, part, half), F32),
            vmem((chips, part, half), F32),
            vmem((chips, part, width), F32),
            vmem((hub_rows, width), F32),
            smem((total,), jnp.int32),
            smem((total,), jnp.int32),
            smem((tiles,), jnp.int32),
            smem((total,), jnp.int32),
            smem((total,), jnp.int32),
            smem((tiles,), jnp.int32),
            dma((12 + nodes // OUT_ROWS,)),
            dma((others,)),
            dma((others,)),
            dma((others,)),
            dma((others,)),
            dma((chips,)),
            dma((chips,)),
            dma((chips,)),
            dma((chips,)),
            dma((chips,)),
            dma((chips,)),
            dma((chips,)),
            dma((chips,)),
            dma((4,)),
            dma((4,)),
        ],
        compiler_params=pltpu.CompilerParams(
            collective_id=0, has_side_effects=True, vmem_limit_bytes=60 * 2**20
        ),
        name="layer",
    )(
        send_tile[0].T,
        recv_count.reshape(peers),
        recv_dst[0].T,
        hub_ids,
        w_self,
        w_neigh,
        bias.reshape(1, width),
        features.reshape(tiles, tile, width),
        hub_adj.reshape(hub_adj.shape[1:]),
        recv_adj.reshape(recv_adj.shape[1:]),
        cotangent.reshape(tiles, tile, width),
    )
    return pl.pallas_call(
        hand_over,
        out_shape=[jax.ShapeDtypeStruct((nodes, width), BF16)] * 2,
        in_specs=[spec(pltpu.HBM)] * 2,
        out_specs=[spec(pltpu.HBM)] * 2,
        scratch_shapes=[vmem((nodes, width), BF16)] * 2 + [dma((2, PIECES))] * 2,
        compiler_params=pltpu.CompilerParams(vmem_limit_bytes=60 * 2**20),
        name="hand_over",
    )(*results)


def solution(mesh):
    placed = (
        P(("row", "col"), None),
        P(),
        P(),
        P(),
        P(),
        P(("row", "col"), None, None, None),
        P(("row", "col"), None, None),
        P(("row", "col"), None),
        P(("row", "col"), None, None),
        P(("row", "col"), None, None, None, None),
        P(("row", "col"), None),
    )
    return jax.shard_map(
        shards,
        mesh=mesh,
        in_specs=placed,
        out_specs=(P(("row", "col"), None), P(("row", "col"), None)),
        check_vma=False,
    )
```
